32 devices in a mesh: blk: 8 (over y, x, core), rep: 4 (over z).
Axes of the slice: x: 2, y: 2, z: 4, core: 2. Of those that a mesh axis runs over, the one named last changes fastest.
Arguments:
- features: bfloat16 [4096, 512], P('blk'), may hold values from -2000 to 2000
- labels: int32 [4096], P('blk'), may hold values from 0 to 127
- w_first: bfloat16 [512, 512], replicated, may hold values from -0.25 to 0.25
- w_second: bfloat16 [512, 128], replicated, may hold values from -0.25 to 0.25
- block_rows: int32 [8, 4, 2, 2], P('blk', 'rep'), may hold values from 0 to 1, as said below
- block_cols: int32 [8, 4, 2, 2], P('blk', 'rep'), may hold values from 0 to 1
- block_vals: bfloat16 [8, 4, 2, 2, 256, 256], P('blk', 'rep')
Outputs:
- logits: bfloat16 [4096, 128], P('blk')
- grad_first: float32 [512, 512], replicated
- grad_second: float32 [512, 128], replicated
- loss: float32 [], replicated
The draws below stay inside these ranges and needn't reach their ends.
Inputs may be any that keep to these rules, and one draw needn't show every extreme that they name: `block_rows`: slot (i, r, t, p) holds a block of shard i's rows against shard (i - r * 2 - t) mod 8's columns; the matrix A assembled from all slots is symmetric; slots whose values are all zero are padding.
All inputs are finite; a program needn't handle non-finite values.
Results may differ from the reference program's by a relative error of at most 0.0083.
Values may be sent and summed in bfloat16 or wider, within the bound.
A program may use at most 64 MiB of HBM per device.

```python
import math
import jax
import jax.numpy as jnp
from jax import lax

C = 128
F = 512
HID = 512
BS = 256
RB = 2
HOPS = 2
PC = 2
SHARDS = 8
REPS = 4
STEPS_DEV = 2
NODES = 4096
GB = 16


def layout(key):
    full = (SHARDS, REPS, STEPS_DEV, PC)
    shard = jnp.broadcast_to(jnp.arange(SHARDS, dtype=jnp.int32)[:, None, None, None], full)
    repl = jnp.broadcast_to(jnp.arange(REPS, dtype=jnp.int32)[None, :, None, None], full)
    stepn = jnp.broadcast_to(jnp.arange(STEPS_DEV, dtype=jnp.int32)[None, None, :, None], full)
    slot = jnp.broadcast_to(jnp.arange(PC, dtype=jnp.int32)[None, None, None, :], full)
    other = (shard - repl * STEPS_DEV - stepn) % SHARDS
    lower = jnp.minimum(shard, other)
    upper = jnp.maximum(shard, other)
    picks = jax.random.randint(jax.random.fold_in(key, 11), (SHARDS, SHARDS, PC), 0, RB)
    live_tab = jax.random.randint(jax.random.fold_in(key, 12), (SHARDS, SHARDS), 0, 4)
    flip_tab = jax.random.randint(jax.random.fold_in(key, 13), (SHARDS,), 0, 2)
    chosen = picks[lower, upper, slot]
    flip = flip_tab[shard]
    diag_cols = jnp.where(flip == 1, slot, RB - 1 - slot)
    rows = jnp.where(shard > other, chosen, slot)
    cols = jnp.where(shard < other, chosen, jnp.where(shard > other, slot, diag_cols))
    live = live_tab[lower, upper] > 0
    return (rows.astype(jnp.int32), cols.astype(jnp.int32), other, live)


def draw_block_rows(key, part):
    rows, cols, other, live = layout(key)
    return rows


def draw_block_cols(key, part):
    rows, cols, other, live = layout(key)
    return cols


def draw_block_vals(key, part):
    rows, cols, other, live = layout(key)
    shard = jnp.broadcast_to(jnp.arange(SHARDS, dtype=jnp.int32)[:, None, None, None], rows.shape)
    grow = shard * RB + rows
    gcol = other * RB + cols
    pair = jnp.minimum(grow, gcol) * GB + jnp.maximum(grow, gcol)
    value_key = jax.random.fold_in(key, 21)
    scale = 1.0 / math.sqrt(SHARDS * BS)

    def one_shard(index):
        pid = pair[index].reshape(-1)
        gr = grow[index].reshape(-1)
        gc = gcol[index].reshape(-1)
        alive = live[index].reshape(-1)
        keys = jax.vmap(lambda p: jax.random.fold_in(value_key, p))(pid)
        blocks = jax.vmap(lambda k: jax.random.normal(k, (BS, BS), jnp.float32))(keys)
        flipped = jnp.swapaxes(blocks, 1, 2)
        sym = (blocks + flipped) * math.sqrt(0.5)
        chosen = jnp.where((gr < gc)[:, None, None], blocks, jnp.where((gr > gc)[:, None, None], flipped, sym))
        chosen = chosen * scale * alive.astype(jnp.float32)[:, None, None]
        return chosen.astype(jnp.bfloat16).reshape(REPS, STEPS_DEV, PC, BS, BS)
    return lax.map(one_shard, jnp.arange(SHARDS, dtype=jnp.int32))


def draw_features(key, part):
    values = jax.random.truncated_normal(jax.random.fold_in(key, 1), -6.0, 6.0, (NODES, F), jnp.float32)
    return values.astype(jnp.bfloat16)


def touch_ends(values, stream_key, least, top_value):
    longest = values.shape.index(max(values.shape))
    spots = []
    for shift in (0, 1):
        where = [jax.random.randint(jax.random.fold_in(stream_key, axis), (), 0, length) for axis, length in enumerate(values.shape)]
        where[longest] = (where[longest] + shift) % values.shape[longest]
        spots.append(tuple(where))
    return values.at[spots[0]].set(least).at[spots[1]].set(top_value)


def normal_values(stream_key, dims, scale, reach, kind=jnp.bfloat16):
    result = scale * jax.random.normal(stream_key, dims, jnp.float32)
    return jnp.clip(result, min=-reach, max=reach).astype(kind)


def setup_inputs(seed: int = 0) -> dict:
    key_list = jax.random.split(jax.random.key(seed), 8)
    features = draw_features(jax.random.fold_in(key_list[7], 71), 0)
    labels = touch_ends(jax.random.randint(key_list[1], (NODES,), 0, C), jax.random.fold_in(key_list[1], 1), 0, C - 1).astype(jnp.int32)
    w_first = normal_values(key_list[2], (F, HID), F ** -0.5, 0.25)
    w_second = normal_values(key_list[3], (HID, C), HID ** -0.5, 0.25)
    block_rows = draw_block_rows(jax.random.fold_in(key_list[7], 71), 0)
    block_cols = draw_block_cols(jax.random.fold_in(key_list[7], 71), 0)
    block_vals = draw_block_vals(jax.random.fold_in(key_list[7], 71), 0)
    return dict(features=features, labels=labels, w_first=w_first, w_second=w_second, block_rows=block_rows, block_cols=block_cols, block_vals=block_vals)


alpha_rate = 0.1

def propagate(panel, block_rows, block_cols, block_vals):
    tiles = panel.reshape(SHARDS * RB, BS, C)
    offsets = jnp.arange(REPS, dtype=jnp.int32)[:, None] * STEPS_DEV + jnp.arange(STEPS_DEV, dtype=jnp.int32)[None, :]

    def one_shard(carry, shard):
        rows = block_rows[shard].reshape(-1)
        cols = block_cols[shard].reshape(-1)
        other = jnp.broadcast_to(((shard - offsets) % SHARDS)[:, :, None], (REPS, STEPS_DEV, PC)).reshape(-1)
        picked = tiles[other * RB + cols]
        blocks = block_vals[shard].reshape(-1, BS, BS)
        prods = jnp.einsum('nab,nbc->nac', blocks.astype(jnp.float32), picked.astype(jnp.float32))
        summed = jax.ops.segment_sum(prods, rows, num_segments=RB)
        return (carry, summed)
    _, outs = lax.scan(one_shard, jnp.zeros((), jnp.int32), jnp.arange(SHARDS, dtype=jnp.int32))
    return outs.reshape(NODES, C)

def reference(features, labels, w_first, w_second, block_rows, block_cols, block_vals):
    hidden = jax.nn.relu(jnp.dot(features, w_first, preferred_element_type=jnp.float32)).astype(jnp.bfloat16)
    base = jnp.dot(hidden, w_second, preferred_element_type=jnp.float32).astype(jnp.bfloat16)
    base32 = base.astype(jnp.float32)
    current = base
    for step in range(HOPS):
        mixed = (1.0 - alpha_rate) * propagate(current, block_rows, block_cols, block_vals) + alpha_rate * base32
        current = mixed.astype(jnp.bfloat16)
    logits = mixed.astype(jnp.bfloat16)
    onehot = (labels[:, None] == jnp.arange(C, dtype=jnp.int32)[None, :]).astype(jnp.float32)
    lse = jax.nn.logsumexp(mixed, axis=1)
    picked = lax.optimization_barrier(jnp.sum(mixed * onehot, axis=1))
    loss = jnp.mean(lse - picked)
    scale = 1.0 / jnp.sqrt(jnp.float32(NODES))
    grad_out = (jax.nn.softmax(mixed, axis=1) - onehot) * scale
    grad_base = alpha_rate * grad_out
    moving = grad_out.astype(jnp.bfloat16)
    for step in range(HOPS):
        nxt = (1.0 - alpha_rate) * propagate(moving, block_rows, block_cols, block_vals)
        if step + 1 < HOPS:
            grad_base = grad_base + alpha_rate * nxt
            moving = nxt.astype(jnp.bfloat16)
        else:
            grad_base = grad_base + nxt
    grad_b = grad_base.astype(jnp.bfloat16)
    grad_second = jnp.dot(hidden.T, grad_b, preferred_element_type=jnp.float32)
    back = jnp.dot(grad_b, w_second.T, preferred_element_type=jnp.float32)
    grad_hidden = jnp.where(hidden > 0, back, 0.0).astype(jnp.bfloat16)
    grad_first = jnp.dot(features.T, grad_hidden, preferred_element_type=jnp.float32)
    return (logits, grad_first, grad_second, loss)
```

```python
import functools
import math

import jax
import jax.numpy as jnp
from jax import lax
from jax.experimental import pallas as pl
from jax.experimental.pallas import tpu as pltpu
from jax.sharding import PartitionSpec as P

HOPS = 2
MESH = pl.DeviceIdType.MESH
F32 = jnp.float32
BF16 = jnp.bfloat16

alpha_rate = 0.1


def dot(a, b, dims=((1,), (0,))):
    return lax.dot_general(a, b, (dims, ((), ())), preferred_element_type=F32)


def graph_kernel(nblk, nrep, finish, *refs):
    feat, lab, w1, w2, brow, bcol, bval = refs[:7]
    if finish:
        logits_o, sums_o, ce_o = refs[7:10]
        refs = refs[10:]
    else:
        logits_o, hidden_o, gb_o, ce_o = refs[7:11]
        refs = refs[11:]
    (hidden, base, onehot, acc, scat_send, scat_recv, panel, piece, red_send, red_recv,
     logit_buf, gb_buf, ce_rep, ce_blk, grads, grads_recv, sums,
     scat_ss, scat_rs, mc_ss, mc_rs, red_ss, red_rs, lg_ss, lg_rs, gb_ss, gb_rs,
     cr_ss, cr_rs, cb_ss, cb_rs, gr_ss, gr_rs, az_ss, az_rs, al_ss, al_rs, ac_ss, ac_rs) = refs
    i = lax.axis_index("blk")
    q = lax.axis_index("rep")
    rows, classes = base.shape
    steps, slots, width = bval.shape[2], bval.shape[3], bval.shape[4]
    share = rows // nrep
    nrb = rows // width
    pending = []

    def copy(src, dst, ss, rs, blk, rep):
        return pltpu.make_async_remote_copy(
            src_ref=src, dst_ref=dst, send_sem=ss, recv_sem=rs,
            device_id=(blk, rep), device_id_type=MESH)

    def send(src, dst, ss, rs, blk, rep):
        one = copy(src, dst, ss, rs, blk, rep)
        one.start()
        pending.append(one)

    def arrived(dst, ss, rs):
        copy(dst, dst, ss, rs, i, q).wait_recv()

    def part_of(r):
        return pl.ds(pl.multiple_of(r * share, share), share)

    def beside(x):
        return jnp.concatenate([x[n * width:(n + 1) * width] for n in range(nrb)], axis=1)

    def placed(totals, prod, out_block, in_block):
        at = jnp.full((width, classes), out_block * nrb + in_block, jnp.int32)
        for n in range(nrb):
            for m in range(nrb):
                term = prod[:, m * classes:(m + 1) * classes]
                totals[n] = totals[n] + jnp.where(at == n * nrb + m, term, 0.0)
        return totals

    mine = part_of(q)

    barrier = pltpu.get_barrier_semaphore()
    everyone = nblk * nrep

    def greet(n, carry):
        pl.semaphore_signal(
            barrier, inc=1,
            device_id=(lax.rem(i + n // nrep, nblk), lax.rem(q + n % nrep, nrep)),
            device_id_type=MESH)
        return carry

    if everyone <= 64:
        for n in range(1, everyone):
            greet(n, 0)
    else:
        lax.fori_loop(1, everyone, greet, 0)

    hidden[...] = jnp.maximum(dot(feat[...], w1[...]), 0.0).astype(BF16)
    base[...] = dot(hidden[...], w2[...]).astype(BF16)
    for t in range(steps):
        totals = [jnp.zeros((width, classes), F32) for _ in range(nrb)]
        wide = beside(base[...])
        for p in range(slots):
            prod = dot(bval[0, 0, t, p], wide, ((0,), (0,)))
            totals = placed(totals, prod, bcol[0, 0, t, p], brow[0, 0, t, p])
        for n in range(nrb):
            scat_send[t, n * width:(n + 1) * width, :] = totals[n].astype(BF16)

    pl.semaphore_wait(barrier, everyone - 1)

    for d in list(range(1, nrep)) + [0]:
        r = lax.rem(q + d, nrep)
        for t in range(steps):
            to = lax.rem(i + 2 * nblk - q * steps - t, nblk)
            src = scat_send.at[t, part_of(r)]
            dst = scat_recv.at[t, d]
            if d == 0 and t == 0:
                own = copy(src, dst, scat_ss.at[t, d], scat_rs.at[t, d], to, r)
                pl.when(q != 0)(own.start)

                @pl.when(q == 0)
                def _():
                    scat_recv[0, 0] = scat_send[0, part_of(r)]
            else:
                send(src, dst, scat_ss.at[t, d], scat_rs.at[t, d], to, r)
    scat_own = own

    classes_down = lax.broadcasted_iota(jnp.int32, (classes, rows), 0)
    onehot[...] = jnp.where(lab[...] == classes_down, 1.0, 0.0).astype(F32).T

    total = jnp.zeros((share, classes), F32)
    for d in range(nrep):
        for t in range(steps):
            dst = scat_recv.at[t, d]
            if d == 0 and t == 0:
                @pl.when(q != 0)
                def _():
                    arrived(scat_recv.at[0, 0], scat_ss.at[0, 0], scat_rs.at[0, 0])
            else:
                arrived(dst, scat_ss.at[t, d], scat_rs.at[t, d])
            total = total + scat_recv[t, d].astype(F32)
    base_part = alpha_rate * base[mine, :].astype(F32)
    mc_own = []

    def spread(k, value):
        piece[k] = value
        for d in list(range(1, nrep)) + [0]:
            r = lax.rem(q + d, nrep)
            for t in range(steps):
                to = lax.rem(i + r * steps + t, nblk)
                dst = panel.at[k, t, mine]
                if d == 0 and t == 0:
                    own = copy(piece.at[k], dst, mc_ss.at[k, t, d], mc_rs.at[k, t, d], to, r)
                    pl.when(q != 0)(own.start)
                    mc_own.append(own)

                    @pl.when(q == 0)
                    def _():
                        panel[k, 0, mine, :] = value
                else:
                    send(piece.at[k], dst, mc_ss.at[k, t, d], mc_rs.at[k, t, d], to, r)

    def multiply(k):
        totals = [jnp.zeros((width, classes), F32) for _ in range(nrb)]
        for t in range(steps):
            for d in range(nrep):
                dst = panel.at[k, t, part_of(lax.rem(q + nrep - d, nrep))]
                if d == 0 and t == 0:
                    @pl.when(q != 0)
                    def _():
                        arrived(dst, mc_ss.at[k, 0, 0], mc_rs.at[k, 0, 0])
                else:
                    arrived(dst, mc_ss.at[k, t, d], mc_rs.at[k, t, d])
            wide = beside(panel[k, t])
            for p in range(slots):
                prod = dot(bval[0, 0, t, p], wide)
                totals = placed(totals, prod, brow[0, 0, t, p], bcol[0, 0, t, p])
        for n in range(nrb):
            acc[n * width:(n + 1) * width, :] = totals[n]
            red_send[k, n * width:(n + 1) * width, :] = totals[n].astype(BF16)
        for d in range(1, nrep):
            r = lax.rem(q + d, nrep)
            send(red_send.at[k, part_of(r)], red_recv.at[k, d],
                 red_ss.at[k, d], red_rs.at[k, d], i, r)
        out = acc[mine, :]
        for d in range(1, nrep):
            arrived(red_recv.at[k, d], red_ss.at[k, d], red_rs.at[k, d])
            out = out + red_recv[k, d].astype(F32)
        return out

    def to_reps(buf, ss, rs):
        for d in range(1, nrep):
            send(buf.at[mine], buf.at[mine], ss.at[d], rs.at[d], i, lax.rem(q + d, nrep))

    def from_reps(buf, ss, rs):
        for d in range(1, nrep):
            arrived(buf.at[part_of(lax.rem(q + nrep - d, nrep))], ss.at[d], rs.at[d])

    spread(0, ((1.0 - alpha_rate) * total + base_part).astype(BF16))
    mixed = (1.0 - alpha_rate) * multiply(0) + base_part
    hot = onehot[mine, :]
    top = jnp.max(mixed, axis=1, keepdims=True)
    exps = jnp.exp(mixed - top)
    norm = jnp.sum(exps, axis=1, keepdims=True)
    grad_out = (exps / norm - hot) * (1.0 / math.sqrt(rows * nblk))
    spread(1, grad_out.astype(BF16))
    logit_buf[mine, :] = mixed.astype(BF16)
    to_reps(logit_buf, lg_ss, lg_rs)
    ce = top + jnp.log(norm) - jnp.sum(mixed * hot, axis=1, keepdims=True)
    ce_rep[0] = jnp.broadcast_to(jnp.sum(ce, axis=0, keepdims=True), ce_rep.shape[1:])
    if finish:
        for d in range(1, nrep):
            send(ce_rep.at[0], ce_rep.at[d], cr_ss.at[d], cr_rs.at[d], i, lax.rem(q + d, nrep))

    step_one = (1.0 - alpha_rate) * multiply(1)
    spread(2, step_one.astype(BF16))
    grad_base = alpha_rate * grad_out + alpha_rate * step_one
    grad_base = grad_base + (1.0 - alpha_rate) * multiply(2)
    grad_b = grad_base.astype(BF16)

    if finish:
        gb_buf[mine, :] = grad_b
        to_reps(gb_buf, gb_ss, gb_rs)
        part = hidden.shape[1] // nrep
        cols = pl.ds(pl.multiple_of(q * part, part), part)
        hid = hidden[:, cols]
        second = w2[cols, :]
        loss = ce_rep[0]
        for d in range(1, nrep):
            arrived(ce_rep.at[d], cr_ss.at[d], cr_rs.at[d])
            loss = loss + ce_rep[d]
        ce_blk[0] = loss
        from_reps(gb_buf, gb_ss, gb_rs)
        gb = gb_buf[...]
        back = dot(gb, second, ((1,), (1,)))
        gh = jnp.where(hid > 0, back, 0.0).astype(BF16)
        fcount = feat.shape[1]
        grads[:fcount, :] = dot(feat[...], gh, ((0,), (0,))).astype(BF16)
        grads[fcount:, :] = dot(hid, gb, ((0,), (0,))).astype(BF16)
        chunk = grads.shape[0] // nblk

        def chunk_of(b):
            return pl.ds(pl.multiple_of(b * chunk, chunk), chunk)

        for e in range(1, nblk):
            to = lax.rem(i + e, nblk)
            send(grads.at[chunk_of(to)], grads_recv.at[e], gr_ss.at[e], gr_rs.at[e], to, q)
        for e in range(1, nblk):
            to = lax.rem(i + e, nblk)
            send(ce_blk.at[0], ce_blk.at[e], cb_ss.at[e], cb_rs.at[e], to, q)
        whole = grads[chunk_of(i), :].astype(F32)
        for e in range(1, nblk):
            arrived(grads_recv.at[e], gr_ss.at[e], gr_rs.at[e])
            whole = whole + grads_recv[e].astype(F32)
        sums[q, chunk_of(i), :] = whole.astype(BF16)
        here = sums.at[q, chunk_of(i)]
        for d in range(1, nrep):
            send(here, here, az_ss.at[d], az_rs.at[d], i, lax.rem(q + d, nrep))
        half = nblk // 2
        partner = i + 1 - 2 * lax.rem(i, 2)
        for d in range(nrep):
            block = sums.at[lax.rem(q + nrep - d, nrep), chunk_of(i)]
            if d:
                arrived(block, az_ss.at[d], az_rs.at[d])
            for e in range(1, half):
                send(block, block, al_ss.at[d, e], al_rs.at[d, e], lax.rem(i + 2 * e, nblk), q)
            send(block, block, ac_ss.at[d, 0], ac_rs.at[d, 0], partner, q)
        for d in range(nrep):
            for e in range(1, half):
                block = sums.at[lax.rem(q + nrep - d, nrep),
                                chunk_of(lax.rem(i + nblk - 2 * e, nblk))]
                arrived(block, al_ss.at[d, e], al_rs.at[d, e])
                send(block, block, ac_ss.at[d, e], ac_rs.at[d, e], partner, q)
        for e in range(1, nblk):
            arrived(ce_blk.at[e], cb_ss.at[e], cb_rs.at[e])
            loss = loss + ce_blk[e]
        ce_o[...] = loss
        from_reps(logit_buf, lg_ss, lg_rs)
        logits_o[...] = logit_buf[...]
        for d in range(nrep):
            for e in range(half):
                block = sums.at[lax.rem(q + nrep - d, nrep),
                                chunk_of(lax.rem(partner + nblk - 2 * e, nblk))]
                arrived(block, ac_ss.at[d, e], ac_rs.at[d, e])
        sums_o[...] = sums[...]
    else:
        gb_o[...] = grad_b
        hidden_o[...] = hidden[...]
        ce_o[...] = ce_rep[0]
        from_reps(logit_buf, lg_ss, lg_rs)
        logits_o[...] = logit_buf[...]

    for one in pending:
        one.wait_send()
    for one in [scat_own] + mc_own:
        pl.when(q != 0)(one.wait_send)


def on_device(features, labels, w_first, w_second, block_rows, block_cols, block_vals):
    rows, fcount = features.shape
    hcount, classes = w_second.shape
    nblk = lax.axis_size("blk")
    nrep = lax.axis_size("rep")
    steps = block_vals.shape[2]
    share = rows // nrep
    nodes = rows * nblk
    tall = fcount + hcount // nrep
    finish = (nblk % 2 == 0 and hcount // nrep == classes and tall % (16 * nblk) == 0)
    chunk = tall // nblk if finish else 16
    tall = tall if finish else 16
    sdma = pltpu.SemaphoreType.DMA
    vmem = pl.BlockSpec(memory_space=pltpu.VMEM)
    smem = pl.BlockSpec(memory_space=pltpu.SMEM)
    if finish:
        outs = [((rows, classes), BF16), ((nrep, tall, classes), BF16), ((8, 128), F32)]
    else:
        outs = [((rows, classes), BF16), ((rows, hcount), BF16), ((share, classes), BF16),
                ((8, 128), F32)]
    back = HOPS + 1
    scratch = [
        pltpu.VMEM((rows, hcount), BF16),
        pltpu.VMEM((rows, classes), BF16),
        pltpu.VMEM((rows, classes), F32),
        pltpu.VMEM((rows, classes), F32),
        pltpu.VMEM((steps, rows, classes), BF16),
        pltpu.VMEM((steps, nrep, share, classes), BF16),
        pltpu.VMEM((back, steps, rows, classes), BF16),
        pltpu.VMEM((back, share, classes), BF16),
        pltpu.VMEM((back, rows, classes), BF16),
        pltpu.VMEM((back, nrep, share, classes), BF16),
        pltpu.VMEM((rows, classes), BF16),
        pltpu.VMEM((rows, classes), BF16),
        pltpu.VMEM((nrep, 8, 128), F32),
        pltpu.VMEM((nblk, 8, 128), F32),
        pltpu.VMEM((tall, classes), BF16),
        pltpu.VMEM((nblk, chunk, classes), BF16),
        pltpu.VMEM((nrep, tall, classes), BF16),
    ]
    for shape in ((steps, nrep), (back, steps, nrep), (back, nrep), (nrep,), (nrep,), (nrep,),
                  (nblk,), (nblk,), (nrep,), (nrep, nblk // 2), (nrep, nblk // 2)):
        scratch += [sdma(shape), sdma(shape)]
    results = pl.pallas_call(
        functools.partial(graph_kernel, nblk, nrep, finish),
        out_shape=[jax.ShapeDtypeStruct(*one) for one in outs],
        in_specs=[vmem, vmem, vmem, vmem, smem, smem, vmem],
        out_specs=[vmem] * len(outs),
        scratch_shapes=scratch,
        compiler_params=pltpu.CompilerParams(
            collective_id=0, has_side_effects=True, vmem_limit_bytes=40 * 1024 * 1024),
    )(features, labels.reshape(1, rows), w_first, w_second, block_rows, block_cols, block_vals)
    if finish:
        logits, sums, ce = results
        grad_first = jnp.swapaxes(sums[:, :fcount], 0, 1).reshape(fcount, hcount).astype(F32)
        grad_second = sums[:, fcount:].reshape(hcount, classes).astype(F32)
        return (logits, grad_first, grad_second, ce[0, 0] / nodes)

    logits, hidden, grad_own, ce = results
    rep_id = lax.axis_index("rep")

    def own(full):
        return lax.dynamic_slice_in_dim(full, rep_id * share, share, 0)

    hidden_own = own(hidden)
    grad_second = dot(hidden_own, grad_own, ((0,), (0,)))
    grad_hidden = jnp.where(hidden_own > 0, dot(grad_own, w_second, ((1,), (1,))), 0.0)
    grad_first = dot(own(features), grad_hidden.astype(BF16), ((0,), (0,)))
    totals = lax.psum((grad_first, grad_second, ce[0, 0]), ("blk", "rep"))
    return (logits, totals[0], totals[1], totals[2] / nodes)


def solution(mesh):
    in_specs = (
        P("blk", None),
        P("blk"),
        P(),
        P(),
        P("blk", "rep", None, None),
        P("blk", "rep", None, None),
        P("blk", "rep", None, None, None, None),
    )
    out_specs = (P("blk", None), P(), P(), P())
    return jax.shard_map(
        on_device, mesh=mesh, in_specs=in_specs, out_specs=out_specs, check_vma=False
    )
```

```python
import functools
import math

import jax
import jax.numpy as jnp
from jax import lax
from jax.experimental import pallas as pl
from jax.experimental.pallas import tpu as pltpu
from jax.sharding import PartitionSpec as P

HOPS = 2
MESH = pl.DeviceIdType.MESH
F32 = jnp.float32
BF16 = jnp.bfloat16

alpha_rate = 0.1


def dot(a, b, dims=((1,), (0,))):
    return lax.dot_general(a, b, (dims, ((), ())), preferred_element_type=F32)


def graph_kernel(nblk, nrep, finish, *refs):
    given = refs[:7]
    if finish:
        logits_o, first_o, second_o, ce_o = refs[7:11]
        refs = refs[11:]
    else:
        logits_o, hidden_o, gb_o, ce_o = refs[7:11]
        refs = refs[11:]
    feat, lab, w1, w2, brow, bcol, bval = refs[:7]
    load_sem, feat_t, hid_t, second_t = refs[7:11]
    loads = [pltpu.make_async_copy(src, dst, load_sem.at[n])
             for n, (src, dst) in enumerate(zip(given, refs[:7]))]
    for n in (0, 2, 3, 6, 4, 5, 1):
        loads[n].start()
    refs = refs[11:]
    (hidden, base, onehot, acc, scat_send, scat_recv, panel, piece, red_send, red_recv,
     logit_buf, gb_buf, ce_rep, ce_blk, grads, grads_recv, sums,
     scat_ss, scat_rs, mc_ss, mc_rs, red_ss, red_rs, lg_ss, lg_rs, gb_ss, gb_rs,
     cr_ss, cr_rs, cb_ss, cb_rs, gr_ss, gr_rs, az_ss, az_rs, al_ss, al_rs, ac_ss, ac_rs) = refs
    i = lax.axis_index("blk")
    q = lax.axis_index("rep")
    rows, classes = base.shape
    steps, slots, width = bval.shape[2], bval.shape[3], bval.shape[4]
    share = rows // nrep
    nrb = rows // width
    pending = []

    def copy(src, dst, ss, rs, blk, rep):
        return pltpu.make_async_remote_copy(
            src_ref=src, dst_ref=dst, send_sem=ss, recv_sem=rs,
            device_id=(blk, rep), device_id_type=MESH)

    def send(src, dst, ss, rs, blk, rep):
        one = copy(src, dst, ss, rs, blk, rep)
        one.start()
        pending.append(one)

    def arrived(dst, ss, rs):
        copy(dst, dst, ss, rs, i, q).wait_recv()

    def part_of(r):
        return pl.ds(pl.multiple_of(r * share, share), share)

    def beside(x):
        return jnp.concatenate([x[n * width:(n + 1) * width] for n in range(nrb)], axis=1)

    def spot(ref, t, p):
        return ref[0, 0, t:t + 1, p:p + 1]

    def placed(totals, prod, out_block, in_block):
        at = jnp.broadcast_to(out_block * nrb + in_block, (width, classes))
        for n in range(nrb):
            for m in range(nrb):
                term = prod[:, m * classes:(m + 1) * classes]
                totals[n] = totals[n] + jnp.where(at == n * nrb + m, term, 0.0)
        return totals

    mine = part_of(q)

    barrier = pltpu.get_barrier_semaphore()
    everyone = nblk * nrep

    def greet(n, carry):
        pl.semaphore_signal(
            barrier, inc=1,
            device_id=(lax.rem(i + n // nrep, nblk), lax.rem(q + n % nrep, nrep)),
            device_id_type=MESH)
        return carry

    if everyone <= 64:
        for n in range(1, everyone):
            greet(n, 0)
    else:
        lax.fori_loop(1, everyone, greet, 0)

    loads[0].wait()
    loads[2].wait()
    hidden[...] = jnp.maximum(dot(feat[...], w1[...]), 0.0).astype(BF16)
    loads[3].wait()
    base[...] = dot(hidden[...], w2[...]).astype(BF16)
    for n in (4, 5, 6):
        loads[n].wait()
    for t in range(steps):
        totals = [jnp.zeros((width, classes), F32) for _ in range(nrb)]
        wide = beside(base[...])
        for p in range(slots):
            prod = dot(bval[0, 0, t, p], wide, ((0,), (0,)))
            totals = placed(totals, prod, spot(bcol, t, p), spot(brow, t, p))
        for n in range(nrb):
            scat_send[t, n * width:(n + 1) * width, :] = totals[n].astype(BF16)

    pl.semaphore_wait(barrier, everyone - 1)

    for d in list(range(1, nrep)) + [0]:
        r = lax.rem(q + d, nrep)
        for t in range(steps):
            to = lax.rem(i + 2 * nblk - q * steps - t, nblk)
            src = scat_send.at[t, part_of(r)]
            dst = scat_recv.at[t, d]
            if d == 0 and t == 0:
                own = copy(src, dst, scat_ss.at[t, d], scat_rs.at[t, d], to, r)
                pl.when(q != 0)(own.start)

                @pl.when(q == 0)
                def _():
                    scat_recv[0, 0] = scat_send[0, part_of(r)]
            else:
                send(src, dst, scat_ss.at[t, d], scat_rs.at[t, d], to, r)
    scat_own = own

    loads[1].wait()
    classes_down = lax.broadcasted_iota(jnp.int32, (classes, rows), 0)
    onehot[...] = jnp.where(lab[...] == classes_down, 1.0, 0.0).astype(F32).T

    total = jnp.zeros((share, classes), F32)
    for d in range(nrep):
        for t in range(steps):
            dst = scat_recv.at[t, d]
            if d == 0 and t == 0:
                @pl.when(q != 0)
                def _():
                    arrived(scat_recv.at[0, 0], scat_ss.at[0, 0], scat_rs.at[0, 0])
            else:
                arrived(dst, scat_ss.at[t, d], scat_rs.at[t, d])
            total = total + scat_recv[t, d].astype(F32)
    base_part = alpha_rate * base[mine, :].astype(F32)
    mc_own = []

    def spread(k, value):
        piece[k] = value
        for d in list(range(1, nrep)) + [0]:
            r = lax.rem(q + d, nrep)
            for t in range(steps):
                to = lax.rem(i + r * steps + t, nblk)
                dst = panel.at[k, t, mine]
                if d == 0 and t == 0:
                    own = copy(piece.at[k], dst, mc_ss.at[k, t, d], mc_rs.at[k, t, d], to, r)
                    pl.when(q != 0)(own.start)
                    mc_own.append(own)

                    @pl.when(q == 0)
                    def _():
                        panel[k, 0, mine, :] = value
                else:
                    send(piece.at[k], dst, mc_ss.at[k, t, d], mc_rs.at[k, t, d], to, r)

    def multiply(k):
        totals = [jnp.zeros((width, classes), F32) for _ in range(nrb)]
        for t in range(steps):
            for d in range(nrep):
                dst = panel.at[k, t, part_of(lax.rem(q + nrep - d, nrep))]
                if d == 0 and t == 0:
                    @pl.when(q != 0)
                    def _():
                        arrived(dst, mc_ss.at[k, 0, 0], mc_rs.at[k, 0, 0])
                else:
                    arrived(dst, mc_ss.at[k, t, d], mc_rs.at[k, t, d])
            wide = beside(panel[k, t])
            for p in range(slots):
                prod = dot(bval[0, 0, t, p], wide)
                totals = placed(totals, prod, spot(brow, t, p), spot(bcol, t, p))
        for n in range(nrb):
            acc[n * width:(n + 1) * width, :] = totals[n]
            red_send[k, n * width:(n + 1) * width, :] = totals[n].astype(BF16)
        for d in range(1, nrep):
            r = lax.rem(q + d, nrep)
            send(red_send.at[k, part_of(r)], red_recv.at[k, d],
                 red_ss.at[k, d], red_rs.at[k, d], i, r)
        out = acc[mine, :]
        for d in range(1, nrep):
            arrived(red_recv.at[k, d], red_ss.at[k, d], red_rs.at[k, d])
            out = out + red_recv[k, d].astype(F32)
        return out

    def to_reps(buf, ss, rs):
        for d in range(1, nrep):
            send(buf.at[mine], buf.at[mine], ss.at[d], rs.at[d], i, lax.rem(q + d, nrep))

    def from_reps(buf, ss, rs):
        for d in range(1, nrep):
            arrived(buf.at[part_of(lax.rem(q + nrep - d, nrep))], ss.at[d], rs.at[d])

    def ahead():
        part = hidden.shape[1] // nrep
        cols = pl.ds(pl.multiple_of(q * part, part), part)
        feat_t[...] = feat[...].T
        hid_t[...] = hidden[:, cols].T
        second_t[...] = w2[cols, :].T

    spread(0, ((1.0 - alpha_rate) * total + base_part).astype(BF16))
    if finish:
        ahead()
    mixed = (1.0 - alpha_rate) * multiply(0) + base_part
    hot = onehot[mine, :]
    top = jnp.max(mixed, axis=1, keepdims=True)
    exps = jnp.exp(mixed - top)
    norm = jnp.sum(exps, axis=1, keepdims=True)
    grad_out = (exps / norm - hot) * (1.0 / math.sqrt(rows * nblk))
    spread(1, grad_out.astype(BF16))
    logit_buf[mine, :] = mixed.astype(BF16)
    ce = top + jnp.log(norm) - jnp.sum(mixed * hot, axis=1, keepdims=True)
    ce_rep[0] = jnp.broadcast_to(jnp.sum(ce, axis=0, keepdims=True), ce_rep.shape[1:])
    if finish:
        for d in range(1, nrep):
            send(ce_rep.at[0], ce_rep.at[d], cr_ss.at[d], cr_rs.at[d], i, lax.rem(q + d, nrep))

    step_one = (1.0 - alpha_rate) * multiply(1)
    spread(2, step_one.astype(BF16))
    grad_base = alpha_rate * grad_out + alpha_rate * step_one
    grad_base = grad_base + (1.0 - alpha_rate) * multiply(2)
    grad_b = grad_base.astype(BF16)

    if finish:
        gb_buf[mine, :] = grad_b
        to_reps(gb_buf, gb_ss, gb_rs)
        part = hidden.shape[1] // nrep
        cols = pl.ds(pl.multiple_of(q * part, part), part)
        hid = hidden[:, cols]
        loss = ce_rep[0]
        for d in range(1, nrep):
            arrived(ce_rep.at[d], cr_ss.at[d], cr_rs.at[d])
            loss = loss + ce_rep[d]
        ce_blk[0] = loss
        from_reps(gb_buf, gb_ss, gb_rs)
        to_reps(logit_buf, lg_ss, lg_rs)
        gb = gb_buf[...]
        back = dot(gb, second_t[...])
        gh = jnp.where(hid > 0, back, 0.0).astype(BF16)
        fcount = feat.shape[1]
        grads[:fcount, :] = dot(feat_t[...], gh).astype(BF16)
        grads[fcount:, :] = dot(hid_t[...], gb).astype(BF16)
        chunk = grads.shape[0] // nblk

        def chunk_of(b):
            return pl.ds(pl.multiple_of(b * chunk, chunk), chunk)

        for e in range(1, nblk):
            to = lax.rem(i + e, nblk)
            send(grads.at[chunk_of(to)], grads_recv.at[e], gr_ss.at[e], gr_rs.at[e], to, q)
        for e in range(1, nblk):
            to = lax.rem(i + e, nblk)
            send(ce_blk.at[0], ce_blk.at[e], cb_ss.at[e], cb_rs.at[e], to, q)
        whole = grads[chunk_of(i), :].astype(F32)
        for e in range(1, nblk):
            arrived(grads_recv.at[e], gr_ss.at[e], gr_rs.at[e])
            whole = whole + grads_recv[e].astype(F32)
        sums[q, chunk_of(i), :] = whole.astype(BF16)
        here = sums.at[q, chunk_of(i)]
        for d in range(1, nrep):
            send(here, here, az_ss.at[d], az_rs.at[d], i, lax.rem(q + d, nrep))
        half = nblk // 2
        partner = i + 1 - 2 * lax.rem(i, 2)
        for d in range(nrep):
            block = sums.at[lax.rem(q + nrep - d, nrep), chunk_of(i)]
            if d:
                arrived(block, az_ss.at[d], az_rs.at[d])
            for e in range(1, half):
                send(block, block, al_ss.at[d, e], al_rs.at[d, e], lax.rem(i + 2 * e, nblk), q)
            send(block, block, ac_ss.at[d, 0], ac_rs.at[d, 0], partner, q)
        for d in range(nrep):
            for e in range(1, half):
                block = sums.at[lax.rem(q + nrep - d, nrep),
                                chunk_of(lax.rem(i + nblk - 2 * e, nblk))]
                arrived(block, al_ss.at[d, e], al_rs.at[d, e])
                send(block, block, ac_ss.at[d, e], ac_rs.at[d, e], partner, q)
        for e in range(1, nblk):
            arrived(ce_blk.at[e], cb_ss.at[e], cb_rs.at[e])
            loss = loss + ce_blk[e]
        ce_o[...] = loss
        from_reps(logit_buf, lg_ss, lg_rs)
        logits_o[...] = logit_buf[...]
        for d in range(nrep):
            for e in range(half):
                block = sums.at[lax.rem(q + nrep - d, nrep),
                                chunk_of(lax.rem(partner + nblk - 2 * e, nblk))]
                arrived(block, ac_ss.at[d, e], ac_rs.at[d, e])
        for r in range(nrep):
            first_o[:, r * part:(r + 1) * part] = sums[r, :fcount]
            second_o[r * part:(r + 1) * part, :] = sums[r, fcount:]
    else:
        to_reps(logit_buf, lg_ss, lg_rs)
        gb_o[...] = grad_b
        hidden_o[...] = hidden[...]
        ce_o[...] = ce_rep[0]
        from_reps(logit_buf, lg_ss, lg_rs)
        logits_o[...] = logit_buf[...]

    for one in pending:
        one.wait_send()
    for one in [scat_own] + mc_own:
        pl.when(q != 0)(one.wait_send)


def on_device(features, labels, w_first, w_second, block_rows, block_cols, block_vals):
    rows, fcount = features.shape
    hcount, classes = w_second.shape
    nblk = lax.axis_size("blk")
    nrep = lax.axis_size("rep")
    steps = block_vals.shape[2]
    share = rows // nrep
    nodes = rows * nblk
    tall = fcount + hcount // nrep
    finish = (nblk % 2 == 0 and hcount // nrep == classes and tall % (16 * nblk) == 0)
    chunk = tall // nblk if finish else 16
    tall = tall if finish else 16
    sdma = pltpu.SemaphoreType.DMA
    vmem = pl.BlockSpec(memory_space=pltpu.VMEM)
    hbm = pl.BlockSpec(memory_space=pltpu.HBM)
    if finish:
        outs = [((rows, classes), BF16), ((fcount, hcount), BF16), ((hcount, classes), BF16),
                ((8, 128), F32)]
    else:
        outs = [((rows, classes), BF16), ((rows, hcount), BF16), ((share, classes), BF16),
                ((8, 128), F32)]
    back = HOPS + 1
    operands = (features, labels.reshape(1, rows), w_first, w_second,
                block_rows, block_cols, block_vals)
    part = hcount // nrep
    scratch = [pltpu.VMEM(one.shape, one.dtype) for one in operands] + [
        sdma((len(operands),)),
        pltpu.VMEM((fcount, rows), BF16),
        pltpu.VMEM((part, rows), BF16),
        pltpu.VMEM((classes, part), BF16),
        pltpu.VMEM((rows, hcount), BF16),
        pltpu.VMEM((rows, classes), BF16),
        pltpu.VMEM((rows, classes), F32),
        pltpu.VMEM((rows, classes), F32),
        pltpu.VMEM((steps, rows, classes), BF16),
        pltpu.VMEM((steps, nrep, share, classes), BF16),
        pltpu.VMEM((back, steps, rows, classes), BF16),
        pltpu.VMEM((back, share, classes), BF16),
        pltpu.VMEM((back, rows, classes), BF16),
        pltpu.VMEM((back, nrep, share, classes), BF16),
        pltpu.VMEM((rows, classes), BF16),
        pltpu.VMEM((rows, classes), BF16),
        pltpu.VMEM((nrep, 8, 128), F32),
        pltpu.VMEM((nblk, 8, 128), F32),
        pltpu.VMEM((tall, classes), BF16),
        pltpu.VMEM((nblk, chunk, classes), BF16),
        pltpu.VMEM((nrep, tall, classes), BF16),
    ]
    for shape in ((steps, nrep), (back, steps, nrep), (back, nrep), (nrep,), (nrep,), (nrep,),
                  (nblk,), (nblk,), (nrep,), (nrep, nblk // 2), (nrep, nblk // 2)):
        scratch += [sdma(shape), sdma(shape)]
    results = pl.pallas_call(
        functools.partial(graph_kernel, nblk, nrep, finish),
        out_shape=[jax.ShapeDtypeStruct(*one) for one in outs],
        in_specs=[hbm] * len(operands),
        out_specs=[vmem] * len(outs),
        scratch_shapes=scratch,
        compiler_params=pltpu.CompilerParams(
            collective_id=0, has_side_effects=True, vmem_limit_bytes=64 * 1024 * 1024 - 65536),
    )(*operands)
    if finish:
        logits, first, second, ce = results
        return (logits, first.astype(F32), second.astype(F32), ce[0, 0] / nodes)

    logits, hidden, grad_own, ce = results
    rep_id = lax.axis_index("rep")

    def own(full):
        return lax.dynamic_slice_in_dim(full, rep_id * share, share, 0)

    hidden_own = own(hidden)
    grad_second = dot(hidden_own, grad_own, ((0,), (0,)))
    grad_hidden = jnp.where(hidden_own > 0, dot(grad_own, w_second, ((1,), (1,))), 0.0)
    grad_first = dot(own(features), grad_hidden.astype(BF16), ((0,), (0,)))
    totals = lax.psum((grad_first, grad_second, ce[0, 0]), ("blk", "rep"))
    return (logits, totals[0], totals[1], totals[2] / nodes)


def solution(mesh):
    in_specs = (
        P("blk", None),
        P("blk"),
        P(),
        P(),
        P("blk", "rep", None, None),
        P("blk", "rep", None, None),
        P("blk", "rep", None, None, None, None),
    )
    out_specs = (P("blk", None), P(), P(), P())
    return jax.shard_map(
        on_device, mesh=mesh, in_specs=in_specs, out_specs=out_specs, check_vma=False
    )
```

```python
import functools
import math

import jax
import jax.numpy as jnp
from jax import lax
from jax.experimental import pallas as pl
from jax.experimental.pallas import tpu as pltpu
from jax.sharding import PartitionSpec as P

HOPS = 2
MESH = pl.DeviceIdType.MESH
F32 = jnp.float32
BF16 = jnp.bfloat16

alpha_rate = 0.1


def dot(a, b, dims=((1,), (0,))):
    return lax.dot_general(a, b, (dims, ((), ())), preferred_element_type=F32)


def graph_kernel(nblk, nrep, finish, *refs):
    given = refs[:7]
    if finish:
        logits_o, first_o, second_o, ce_o = refs[7:11]
        refs = refs[11:]
    else:
        logits_o, hidden_o, gb_o, ce_o = refs[7:11]
        refs = refs[11:]
    feat, lab, w1, w2, brow, bcol, bval = refs[:7]
    load_sem, feat_t, hid_t, second_t = refs[7:11]
    loads = [pltpu.make_async_copy(src, dst, load_sem.at[n])
             for n, (src, dst) in enumerate(zip(given, refs[:7]))]
    for n in (0, 2, 3, 6, 4, 5, 1):
        loads[n].start()
    refs = refs[11:]
    (hidden, base, onehot, acc, scat_send, scat_recv, panel, piece, red_send, red_recv,
     logit_buf, gb_buf, ce_rep, ce_blk, grads, grads_recv, sums,
     scat_ss, scat_rs, mc_ss, mc_rs, red_ss, red_rs, lg_ss, lg_rs, gb_ss, gb_rs,
     cr_ss, cr_rs, cb_ss, cb_rs, gr_ss, gr_rs, az_ss, az_rs, al_ss, al_rs, ac_ss, ac_rs) = refs
    i = lax.axis_index("blk")
    q = lax.axis_index("rep")
    rows, classes = base.shape
    steps, slots, width = bval.shape[2], bval.shape[3], bval.shape[4]
    share = rows // nrep
    nrb = rows // width
    pending = []

    def copy(src, dst, ss, rs, blk, rep):
        return pltpu.make_async_remote_copy(
            src_ref=src, dst_ref=dst, send_sem=ss, recv_sem=rs,
            device_id=(blk, rep), device_id_type=MESH)

    def send(src, dst, ss, rs, blk, rep):
        one = copy(src, dst, ss, rs, blk, rep)
        one.start()
        pending.append(one)

    def arrived(dst, ss, rs):
        copy(dst, dst, ss, rs, i, q).wait_recv()

    def part_of(r):
        return pl.ds(pl.multiple_of(r * share, share), share)

    def beside(x):
        return jnp.concatenate([x[n * width:(n + 1) * width] for n in range(nrb)], axis=1)

    def spot(ref, t, p):
        return ref[0, 0, t:t + 1, p:p + 1]

    def placed(totals, prod, out_block, in_block):
        at = jnp.broadcast_to(out_block * nrb + in_block, (width, classes))
        for n in range(nrb):
            for m in range(nrb):
                term = prod[:, m * classes:(m + 1) * classes]
                totals[n] = totals[n] + jnp.where(at == n * nrb + m, term, 0.0)
        return totals

    mine = part_of(q)

    barrier = pltpu.get_barrier_semaphore()
    everyone = nblk * nrep

    def greet(n, carry):
        pl.semaphore_signal(
            barrier, inc=1,
            device_id=(lax.rem(i + n // nrep, nblk), lax.rem(q + n % nrep, nrep)),
            device_id_type=MESH)
        return carry

    if everyone <= 64:
        for n in range(1, everyone):
            greet(n, 0)
    else:
        lax.fori_loop(1, everyone, greet, 0)

    loads[0].wait()
    loads[2].wait()
    hidden[...] = jnp.maximum(dot(feat[...], w1[...]), 0.0).astype(BF16)
    loads[3].wait()
    base[...] = dot(hidden[...], w2[...]).astype(BF16)
    for n in (4, 5, 6):
        loads[n].wait()
    for t in range(steps):
        totals = [jnp.zeros((width, classes), F32) for _ in range(nrb)]
        wide = beside(base[...])
        for p in range(slots):
            prod = dot(bval[0, 0, t, p], wide, ((0,), (0,)))
            totals = placed(totals, prod, spot(bcol, t, p), spot(brow, t, p))
        for n in range(nrb):
            scat_send[t, n * width:(n + 1) * width, :] = totals[n].astype(BF16)

    pl.semaphore_wait(barrier, everyone - 1)

    for d in list(range(1, nrep)) + [0]:
        r = lax.rem(q + d, nrep)
        for t in range(steps):
            to = lax.rem(i + 2 * nblk - q * steps - t, nblk)
            src = scat_send.at[t, part_of(r)]
            dst = scat_recv.at[t, d]
            if d == 0 and t == 0:
                own = copy(src, dst, scat_ss.at[t, d], scat_rs.at[t, d], to, r)
                pl.when(q != 0)(own.start)

                @pl.when(q == 0)
                def _():
                    scat_recv[0, 0] = scat_send[0, part_of(r)]
            else:
                send(src, dst, scat_ss.at[t, d], scat_rs.at[t, d], to, r)
    scat_own = own

    loads[1].wait()
    classes_down = lax.broadcasted_iota(jnp.int32, (classes, rows), 0)
    onehot[...] = jnp.where(lab[...] == classes_down, 1.0, 0.0).astype(F32).T

    total = jnp.zeros((share, classes), F32)
    for d in range(nrep):
        for t in range(steps):
            dst = scat_recv.at[t, d]
            if d == 0 and t == 0:
                @pl.when(q != 0)
                def _():
                    arrived(scat_recv.at[0, 0], scat_ss.at[0, 0], scat_rs.at[0, 0])
            else:
                arrived(dst, scat_ss.at[t, d], scat_rs.at[t, d])
            total = total + scat_recv[t, d].astype(F32)
    base_part = alpha_rate * base[mine, :].astype(F32)
    mc_own = []

    def spread(k, value):
        piece[k] = value
        for d in list(range(1, nrep)) + [0]:
            r = lax.rem(q + d, nrep)
            to = lax.rem(i + r * steps, nblk)
            dst = panel.at[k, 0, mine]
            if d == 0:
                own = copy(piece.at[k], dst, mc_ss.at[k, 0, 0], mc_rs.at[k, 0, 0], to, r)
                pl.when(q != 0)(own.start)
                mc_own.append(own)

                @pl.when(q == 0)
                def _():
                    panel[k, 0, mine, :] = value
            else:
                send(piece.at[k], dst, mc_ss.at[k, 0, d], mc_rs.at[k, 0, d], to, r)

    def multiply(k):
        totals = [jnp.zeros((width, classes), F32) for _ in range(nrb)]
        for t in range(steps):
            for d in range(nrep):
                dst = panel.at[k, t, part_of(lax.rem(q + nrep - d, nrep))]
                if d == 0 and t == 0:
                    @pl.when(q != 0)
                    def _():
                        arrived(dst, mc_ss.at[k, 0, 0], mc_rs.at[k, 0, 0])
                else:
                    arrived(dst, mc_ss.at[k, t, d], mc_rs.at[k, t, d])
                if t + 1 < steps:
                    rows_of = part_of(lax.rem(q + nrep - d, nrep))
                    send(dst, panel.at[k, t + 1, rows_of], mc_ss.at[k, t + 1, d],
                         mc_rs.at[k, t + 1, d], lax.rem(i + 1, nblk), q)
            wide = beside(panel[k, t])
            for p in range(slots):
                prod = dot(bval[0, 0, t, p], wide)
                totals = placed(totals, prod, spot(brow, t, p), spot(bcol, t, p))
        for n in range(nrb):
            acc[n * width:(n + 1) * width, :] = totals[n]
            red_send[k, n * width:(n + 1) * width, :] = totals[n].astype(BF16)
        for d in range(1, nrep):
            r = lax.rem(q + d, nrep)
            send(red_send.at[k, part_of(r)], red_recv.at[k, d],
                 red_ss.at[k, d], red_rs.at[k, d], i, r)
        out = acc[mine, :]
        for d in range(1, nrep):
            arrived(red_recv.at[k, d], red_ss.at[k, d], red_rs.at[k, d])
            out = out + red_recv[k, d].astype(F32)
        return out

    def to_reps(buf, ss, rs):
        for d in range(1, nrep):
            send(buf.at[mine], buf.at[mine], ss.at[d], rs.at[d], i, lax.rem(q + d, nrep))

    def from_reps(buf, ss, rs):
        for d in range(1, nrep):
            arrived(buf.at[part_of(lax.rem(q + nrep - d, nrep))], ss.at[d], rs.at[d])

    def ahead():
        part = hidden.shape[1] // nrep
        cols = pl.ds(pl.multiple_of(q * part, part), part)
        feat_t[...] = feat[...].T
        hid_t[...] = hidden[:, cols].T
        second_t[...] = w2[cols, :].T

    spread(0, ((1.0 - alpha_rate) * total + base_part).astype(BF16))
    if finish:
        ahead()
    mixed = (1.0 - alpha_rate) * multiply(0) + base_part
    hot = onehot[mine, :]
    top = jnp.max(mixed, axis=1, keepdims=True)
    exps = jnp.exp(mixed - top)
    norm = jnp.sum(exps, axis=1, keepdims=True)
    grad_out = (exps / norm - hot) * (1.0 / math.sqrt(rows * nblk))
    spread(1, grad_out.astype(BF16))
    logit_buf[mine, :] = mixed.astype(BF16)
    ce = top + jnp.log(norm) - jnp.sum(mixed * hot, axis=1, keepdims=True)
    ce_rep[0] = jnp.broadcast_to(jnp.sum(ce, axis=0, keepdims=True), ce_rep.shape[1:])
    if finish:
        for d in range(1, nrep):
            send(ce_rep.at[0], ce_rep.at[d], cr_ss.at[d], cr_rs.at[d], i, lax.rem(q + d, nrep))

    step_one = (1.0 - alpha_rate) * multiply(1)
    spread(2, step_one.astype(BF16))
    grad_base = alpha_rate * grad_out + alpha_rate * step_one
    grad_base = grad_base + (1.0 - alpha_rate) * multiply(2)
    grad_b = grad_base.astype(BF16)

    if finish:
        gb_buf[mine, :] = grad_b
        to_reps(gb_buf, gb_ss, gb_rs)
        part = hidden.shape[1] // nrep
        cols = pl.ds(pl.multiple_of(q * part, part), part)
        hid = hidden[:, cols]
        loss = ce_rep[0]
        for d in range(1, nrep):
            arrived(ce_rep.at[d], cr_ss.at[d], cr_rs.at[d])
            loss = loss + ce_rep[d]
        ce_blk[0] = loss
        from_reps(gb_buf, gb_ss, gb_rs)
        to_reps(logit_buf, lg_ss, lg_rs)
        gb = gb_buf[...]
        back = dot(gb, second_t[...])
        gh = jnp.where(hid > 0, back, 0.0).astype(BF16)
        fcount = feat.shape[1]
        grads[:fcount, :] = dot(feat_t[...], gh).astype(BF16)
        grads[fcount:, :] = dot(hid_t[...], gb).astype(BF16)
        chunk = grads.shape[0] // nblk

        def chunk_of(b):
            return pl.ds(pl.multiple_of(b * chunk, chunk), chunk)

        for e in range(1, nblk):
            to = lax.rem(i + e, nblk)
            send(grads.at[chunk_of(to)], grads_recv.at[e], gr_ss.at[e], gr_rs.at[e], to, q)
        for e in range(1, nblk):
            to = lax.rem(i + e, nblk)
            send(ce_blk.at[0], ce_blk.at[e], cb_ss.at[e], cb_rs.at[e], to, q)
        whole = grads[chunk_of(i), :].astype(F32)
        for e in range(1, nblk):
            arrived(grads_recv.at[e], gr_ss.at[e], gr_rs.at[e])
            whole = whole + grads_recv[e].astype(F32)
        sums[q, chunk_of(i), :] = whole.astype(BF16)
        here = sums.at[q, chunk_of(i)]
        for d in range(1, nrep):
            send(here, here, az_ss.at[d], az_rs.at[d], i, lax.rem(q + d, nrep))
        half = nblk // 2
        partner = i + 1 - 2 * lax.rem(i, 2)
        for d in range(nrep):
            block = sums.at[lax.rem(q + nrep - d, nrep), chunk_of(i)]
            if d:
                arrived(block, az_ss.at[d], az_rs.at[d])
            for e in range(1, half):
                send(block, block, al_ss.at[d, e], al_rs.at[d, e], lax.rem(i + 2 * e, nblk), q)
            send(block, block, ac_ss.at[d, 0], ac_rs.at[d, 0], partner, q)
        for d in range(nrep):
            for e in range(1, half):
                block = sums.at[lax.rem(q + nrep - d, nrep),
                                chunk_of(lax.rem(i + nblk - 2 * e, nblk))]
                arrived(block, al_ss.at[d, e], al_rs.at[d, e])
                send(block, block, ac_ss.at[d, e], ac_rs.at[d, e], partner, q)
        for e in range(1, nblk):
            arrived(ce_blk.at[e], cb_ss.at[e], cb_rs.at[e])
            loss = loss + ce_blk[e]
        ce_o[...] = loss[:1, :1] * (1.0 / (rows * nblk))
        from_reps(logit_buf, lg_ss, lg_rs)
        logits_o[...] = logit_buf[...]
        for d in range(nrep):
            for e in range(half):
                block = sums.at[lax.rem(q + nrep - d, nrep),
                                chunk_of(lax.rem(partner + nblk - 2 * e, nblk))]
                arrived(block, ac_ss.at[d, e], ac_rs.at[d, e])
        for r in range(nrep):
            first_o[:, r * part:(r + 1) * part] = sums[r, :fcount].astype(F32)
            second_o[r * part:(r + 1) * part, :] = sums[r, fcount:].astype(F32)
    else:
        to_reps(logit_buf, lg_ss, lg_rs)
        gb_o[...] = grad_b
        hidden_o[...] = hidden[...]
        ce_o[...] = ce_rep[0]
        from_reps(logit_buf, lg_ss, lg_rs)
        logits_o[...] = logit_buf[...]

    for one in pending:
        one.wait_send()
    for one in [scat_own] + mc_own:
        pl.when(q != 0)(one.wait_send)


def on_device(features, labels, w_first, w_second, block_rows, block_cols, block_vals):
    rows, fcount = features.shape
    hcount, classes = w_second.shape
    nblk = lax.axis_size("blk")
    nrep = lax.axis_size("rep")
    steps = block_vals.shape[2]
    share = rows // nrep
    nodes = rows * nblk
    tall = fcount + hcount // nrep
    finish = (nblk % 2 == 0 and hcount // nrep == classes and tall % (16 * nblk) == 0)
    chunk = tall // nblk if finish else 16
    tall = tall if finish else 16
    sdma = pltpu.SemaphoreType.DMA
    vmem = pl.BlockSpec(memory_space=pltpu.VMEM)
    hbm = pl.BlockSpec(memory_space=pltpu.HBM)
    if finish:
        outs = [((rows, classes), BF16), ((fcount, hcount), F32), ((hcount, classes), F32),
                ((1, 1), F32)]
    else:
        outs = [((rows, classes), BF16), ((rows, hcount), BF16), ((share, classes), BF16),
                ((8, 128), F32)]
    back = HOPS + 1
    operands = (features, labels.reshape(1, rows), w_first, w_second,
                block_rows, block_cols, block_vals)
    part = hcount // nrep
    scratch = [pltpu.VMEM(one.shape, one.dtype) for one in operands] + [
        sdma((len(operands),)),
        pltpu.VMEM((fcount, rows), BF16),
        pltpu.VMEM((part, rows), BF16),
        pltpu.VMEM((classes, part), BF16),
        pltpu.VMEM((rows, hcount), BF16),
        pltpu.VMEM((rows, classes), BF16),
        pltpu.VMEM((rows, classes), F32),
        pltpu.VMEM((rows, classes), F32),
        pltpu.VMEM((steps, rows, classes), BF16),
        pltpu.VMEM((steps, nrep, share, classes), BF16),
        pltpu.VMEM((back, steps, rows, classes), BF16),
        pltpu.VMEM((back, share, classes), BF16),
        pltpu.VMEM((back, rows, classes), BF16),
        pltpu.VMEM((back, nrep, share, classes), BF16),
        pltpu.VMEM((rows, classes), BF16),
        pltpu.VMEM((rows, classes), BF16),
        pltpu.VMEM((nrep, 8, 128), F32),
        pltpu.VMEM((nblk, 8, 128), F32),
        pltpu.VMEM((tall, classes), BF16),
        pltpu.VMEM((nblk, chunk, classes), BF16),
        pltpu.VMEM((nrep, tall, classes), BF16),
    ]
    for shape in ((steps, nrep), (back, steps, nrep), (back, nrep), (nrep,), (nrep,), (nrep,),
                  (nblk,), (nblk,), (nrep,), (nrep, nblk // 2), (nrep, nblk // 2)):
        scratch += [sdma(shape), sdma(shape)]
    results = pl.pallas_call(
        functools.partial(graph_kernel, nblk, nrep, finish),
        out_shape=[jax.ShapeDtypeStruct(*one) for one in outs],
        in_specs=[hbm] * len(operands),
        out_specs=[vmem] * len(outs),
        scratch_shapes=scratch,
        compiler_params=pltpu.CompilerParams(
            collective_id=0, has_side_effects=True, vmem_limit_bytes=64 * 1024 * 1024 - 65536),
    )(*operands)
    if finish:
        logits, first, second, ce = results
        return (logits, first, second, ce.reshape(()))

    logits, hidden, grad_own, ce = results
    rep_id = lax.axis_index("rep")

    def own(full):
        return lax.dynamic_slice_in_dim(full, rep_id * share, share, 0)

    hidden_own = own(hidden)
    grad_second = dot(hidden_own, grad_own, ((0,), (0,)))
    grad_hidden = jnp.where(hidden_own > 0, dot(grad_own, w_second, ((1,), (1,))), 0.0)
    grad_first = dot(own(features), grad_hidden.astype(BF16), ((0,), (0,)))
    totals = lax.psum((grad_first, grad_second, ce[0, 0]), ("blk", "rep"))
    return (logits, totals[0], totals[1], totals[2] / nodes)


def solution(mesh):
    in_specs = (
        P("blk", None),
        P("blk"),
        P(),
        P(),
        P("blk", "rep", None, None),
        P("blk", "rep", None, None),
        P("blk", "rep", None, None, None, None),
    )
    out_specs = (P("blk", None), P(), P(), P())
    return jax.shard_map(
        on_device, mesh=mesh, in_specs=in_specs, out_specs=out_specs, check_vma=False
    )
```
